32 devices in a mesh: group: 2 (over x), turb: 16 (over z, y, core).
Axes of the slice: x: 2, y: 2, z: 4, core: 2. Of those that a mesh axis runs over, the one named last changes fastest.
Arguments:
- incident: float32 [32, 2, 64, 1024], P(('group', 'turb')), parts along dimension 0, may hold values from -6 to 6
- self_block_inverse: bfloat16 [32, 2, 1024, 1024], P(('group', 'turb')), parts along dimension 0, may hold values from -0.125 to 0.125
- couplings: bfloat16 [32, 5, 2, 1024, 1024], P(('group', 'turb')), parts along dimension 0, may hold values from -0.03125 to 0.03125
- partners: int32 [32, 5], P(('group', 'turb')), parts along dimension 0, may hold values from -1 to 14, as said below
- basis_count: int32 [32], P(('group', 'turb')), parts along dimension 0, may hold values from 512 to 1024
Outputs:
- coefficients: float32 [32, 2, 64, 1024], P(('group', 'turb')), parts along dimension 0
The draws below stay inside these ranges and needn't reach their ends.
There are 2 independent parts, one for each index of `group`. The reference program is written for one: setup_inputs(seed, part) draws one part's arguments, and reference() takes and returns one part's arrays. A program takes and returns all parts, laid end to end along the dimension named above; each array names one. Nothing has to cross between parts.
Inputs may be any that keep to these rules, and one draw needn't show every extreme that they name: `partners`: each live entry s of row t satisfies t - 8 <= s < t; the entries of a row are distinct, so each unordered pair is listed once; the block of an empty slot is unused; some turbine has a partner at exactly t - 8 and some turbine fills all 5 slots.
All inputs are finite; a program needn't handle non-finite values.
Results may differ from the reference program's by a relative error of at most 0.008.
Values may be sent and summed in bfloat16 or wider, within the bound.
A program may use at most 192 MiB of HBM per device.

```python
import jax
import jax.numpy as jnp
from jax import lax

BASIS_FUNCTIONS = 1024
INCIDENT_WAVES = 64
PAIR_SLOTS = 5
REACH = 8
ITERS = 2
FARM_TURBINES = 16


def draw_partners(key, part):
    key = jax.random.fold_in(key, 7)
    perm_key, count_key = jax.random.split(key)
    row_keys = jax.random.split(perm_key, FARM_TURBINES)
    orders = jax.vmap(lambda one_key: jax.random.permutation(one_key, REACH))(row_keys) + 1
    offsets = orders[:, :PAIR_SLOTS].astype(jnp.int32)
    fixed_row = jnp.where(jnp.arange(PAIR_SLOTS) == 0, REACH, jnp.arange(PAIR_SLOTS)).astype(jnp.int32)
    offsets = offsets.at[FARM_TURBINES - 1].set(fixed_row)
    live_count = jax.random.randint(count_key, (FARM_TURBINES,), 0, PAIR_SLOTS + 1).astype(jnp.int32)
    live_count = live_count.at[FARM_TURBINES - 1].set(PAIR_SLOTS)
    slot_ids = jnp.arange(PAIR_SLOTS, dtype=jnp.int32)
    partner = jnp.arange(FARM_TURBINES, dtype=jnp.int32)[:, None] - offsets
    valid = (slot_ids[None, :] < live_count[:, None]) & (partner >= 0)
    return jnp.where(valid, partner, -1).astype(jnp.int32)


def with_ends(drawn, own_key, low, largest):
    place = [jax.random.randint(jax.random.fold_in(own_key, axis), (), 0, length) for axis, length in enumerate(drawn.shape)]
    longest = drawn.shape.index(max(drawn.shape))
    beside = place[:longest] + [(place[longest] + 1) % drawn.shape[longest]] + place[longest + 1:]
    return drawn.at[tuple(place)].set(low).at[tuple(beside)].set(largest)


def shard_levels(rng, dims, shards, smallest, high):
    loudness, own = 1.0, jax.random.fold_in(rng, 6)
    for position, blocks in shards:
        draws = jnp.exp(jax.random.uniform(jax.random.fold_in(own, position), (blocks,), jnp.float32, smallest / len(shards), high / len(shards)))
        loudness = loudness * jnp.repeat(draws, dims[position] // blocks).reshape([-1 if axis == position else 1 for axis in range(len(dims))])
    return loudness


def noise(own_key, shape, deviation, bound, pieces=(), held_as=jnp.bfloat16):
    level = shard_levels(own_key, shape, pieces, -0.22, 0.18) if pieces else 1.0
    drawn = jax.random.normal(own_key, shape, jnp.float32) * deviation * level
    return jnp.minimum(jnp.maximum(drawn, -bound), bound).astype(held_as)


def setup_inputs(seed: int = 0, part: int = 0) -> dict:
    keys = jax.random.split(jax.random.key(seed), 6)
    part_keys = jax.random.split(jax.random.fold_in(keys[5], part), 6)
    incident = noise(part_keys[0], (FARM_TURBINES, 2, INCIDENT_WAVES, BASIS_FUNCTIONS), 1.0, 6.0, ((0, 16),), jnp.float32)
    self_block_inverse = noise(part_keys[1], (FARM_TURBINES, 2, BASIS_FUNCTIONS, BASIS_FUNCTIONS), (2 * BASIS_FUNCTIONS) ** -0.5, 0.125, ((0, 16),))
    couplings = noise(part_keys[2], (FARM_TURBINES, PAIR_SLOTS, 2, BASIS_FUNCTIONS, BASIS_FUNCTIONS), (32 * BASIS_FUNCTIONS) ** -0.5, 0.03125, ((0, 16),))
    partners = draw_partners(jax.random.fold_in(jax.random.fold_in(keys[5], part), 71), part)
    basis_count = with_ends(jax.random.randint(part_keys[4], (FARM_TURBINES,), BASIS_FUNCTIONS // 2, BASIS_FUNCTIONS + 1), jax.random.fold_in(part_keys[4], 1), BASIS_FUNCTIONS // 2, BASIS_FUNCTIONS).astype(jnp.int32)
    return {"incident": incident, "self_block_inverse": self_block_inverse, "couplings": couplings, "partners": partners, "basis_count": basis_count}


def complex_rows(coeffs, block, flipped):
    rows = coeffs.shape[1]
    stacked = coeffs.reshape(2 * rows, coeffs.shape[2])
    if flipped:
        first = jnp.dot(stacked, block[0], preferred_element_type=jnp.float32)
        second = jnp.dot(stacked, block[1], preferred_element_type=jnp.float32)
    else:
        first = jnp.dot(stacked, block[0].T, preferred_element_type=jnp.float32)
        second = jnp.dot(stacked, block[1].T, preferred_element_type=jnp.float32)
    real_part = first[:rows] - second[rows:]
    imag_part = second[:rows] + first[rows:]
    return jnp.stack([real_part, imag_part])


def reference(incident, self_block_inverse, couplings, partners, basis_count):
    turbine_positions = jnp.arange(BASIS_FUNCTIONS, dtype=jnp.int32)
    active_mask = (turbine_positions[None, :] < basis_count[:, None]).astype(jnp.float32)[:, None, None, :]

    def solve_all(right):
        return lax.map(lambda pair: complex_rows(pair[0], pair[1], False), (right, self_block_inverse))

    coefficients = active_mask * solve_all(incident.astype(jnp.bfloat16))
    for sweep in range(ITERS):
        rounded = coefficients.astype(jnp.bfloat16)

        def per_turbine(packed):
            row, own_coeff, blocks = packed
            valid = row >= 0
            safe_rows = jnp.maximum(row, 0).astype(jnp.int32)
            partner_coeffs = rounded[safe_rows]
            forward_coupling = jnp.zeros((2, INCIDENT_WAVES, BASIS_FUNCTIONS), jnp.float32)
            backs = []
            for slot_index in range(PAIR_SLOTS):
                ahead = complex_rows(partner_coeffs[slot_index], blocks[slot_index], False)
                forward_coupling = forward_coupling + jnp.where(valid[slot_index], ahead, jnp.zeros_like(ahead))
                behind = complex_rows(own_coeff, blocks[slot_index], True)
                backs.append(jnp.where(valid[slot_index], behind, jnp.zeros_like(behind)))
            return forward_coupling, jnp.stack(backs)

        forward_coupling, backward_coupling = lax.map(per_turbine, (partners, rounded, couplings))
        target_turbines = jnp.maximum(partners, 0).astype(jnp.int32).reshape(-1)
        incoming_field = jnp.zeros((FARM_TURBINES, 2, INCIDENT_WAVES, BASIS_FUNCTIONS), jnp.float32).at[target_turbines].add(backward_coupling.reshape(-1, 2, INCIDENT_WAVES, BASIS_FUNCTIONS))
        coupling = forward_coupling + incoming_field
        right = (incident - coupling).astype(jnp.bfloat16)
        coefficients = active_mask * solve_all(right)
    return coefficients
```

```python
import functools

import jax
import jax.numpy as jnp
from jax import lax
from jax.experimental import pallas as pl
from jax.experimental.pallas import tpu as pltpu
from jax.sharding import PartitionSpec as P

ITERS = 2
REACH = 8
TILE = 256
MESH = pl.DeviceIdType.MESH
NT = (((1,), (1,)), ((), ()))
NN = (((1,), (0,)), ((), ()))


def kernel(
    n,
    partners_ref, count_ref, incident_ref, inverse_hbm, couplings_hbm, out_ref,
    inverse, couplings, own_u, own_v, fields, turned, staged_u, staged_v, right_u, right_v, behind,
    got0, got1, parts0, parts1, mated0, mated1, below0, below1, across0, across1,
    load_sem, send_sem, got_sem, mated_sem, below_sem, across_sem,
):
    slots = couplings_hbm.shape[0]
    height, width = incident_ref.shape
    half = height // 2
    tiles = width // TILE
    me = lax.axis_index("turb")
    core = lax.rem(me, 2)
    odd_chip = lax.rem(me // 2, 2)
    mate = me + 1 - 2 * core
    pair = me + 2 - 4 * odd_chip
    has_up = me + 4 < n
    has_down = me >= 4
    up = jnp.where(has_up, me + 4, me)
    down = jnp.where(has_down, me - 4, me)
    got, parts, mated = (got0, got1), (parts0, parts1), (mated0, mated1)
    below, across = (below0, below1), (across0, across1)

    load_inverse = pltpu.make_async_copy(inverse_hbm, inverse, load_sem.at[slots])
    load_inverse.start()
    for j in range(slots):
        pltpu.make_async_copy(couplings_hbm.at[j], couplings.at[j], load_sem.at[j]).start()

    empty = jnp.zeros((height, width), jnp.bfloat16)
    for sweep in range(ITERS):
        for o in range(REACH + 1):
            got[sweep][o] = empty
        mated[sweep][0] = empty
        mated[sweep][4] = empty
        below[sweep][2] = empty
    behind[slots] = empty

    barrier = pltpu.get_barrier_semaphore()

    def greet(other):
        pl.semaphore_signal(barrier, inc=1, device_id={"turb": other}, device_id_type=MESH)

    greet(mate)
    greet(pair)
    pl.when(has_up)(lambda: greet(up))
    pl.when(has_down)(lambda: greet(down))

    count = count_ref[0]
    offsets = []
    for j in range(slots):
        partner = partners_ref[0, j]
        offsets.append(jnp.clip(jnp.where(partner >= 0, me - partner, 0), 0, REACH))
    listed = []
    for o in range(1, REACH + 1):
        place = jnp.int32(slots)
        for j in range(slots):
            place = jnp.where(offsets[j] == o, j, place)
        listed.append(place)

    def columns(c):
        return pl.ds(pl.multiple_of(c * TILE, TILE), TILE)

    def solve(u, v, u_out, v_out, last):
        @pl.loop(0, tiles)
        def _(c):
            cols = columns(c)
            acc = lax.dot_general(u[...], inverse[0, cols, :], NT, preferred_element_type=jnp.float32)
            acc += lax.dot_general(v[...], inverse[1, cols, :], NT, preferred_element_type=jnp.float32)
            position = lax.broadcasted_iota(jnp.int32, (height, TILE), 1) + c * TILE
            acc = acc * (position < count).astype(jnp.float32)
            if last:
                out_ref[:, cols] = acc
            else:
                rounded = acc.astype(jnp.bfloat16)
                u_out[:, cols] = rounded
                v_out[:half, cols] = -rounded[half:]
                v_out[half:, cols] = rounded[:half]

    first = incident_ref[...].astype(jnp.bfloat16)
    right_u[...] = first
    right_v[:half] = -first[half:]
    right_v[half:] = first[:half]
    load_inverse.wait()
    solve(right_u, right_v, own_u.at[0], own_v, False)
    pl.semaphore_wait(barrier, 2 + has_up.astype(jnp.int32) + has_down.astype(jnp.int32))

    sent = []

    def send(sweep, number, src, dst, arrival, device, cond=None):
        copy = pltpu.make_async_remote_copy(
            src_ref=src, dst_ref=dst, send_sem=send_sem.at[sweep, number], recv_sem=arrival,
            device_id={"turb": device}, device_id_type=MESH,
        )
        sent.append((copy, cond))
        if cond is None:
            copy.start()
        else:
            pl.when(cond)(copy.start)

    def arrived(dst, arrival, cond=None):
        copy = pltpu.make_async_remote_copy(
            src_ref=dst, dst_ref=dst, send_sem=send_sem.at[0, 0], recv_sem=arrival,
            device_id={"turb": mate}, device_id_type=MESH,
        )
        if cond is None:
            copy.wait_recv()
        else:
            pl.when(cond)(copy.wait_recv)

    even_core, even_chip = core == 0, odd_chip == 0
    for sweep in range(ITERS):
        block, part, mates, lows, over = got[sweep], parts[sweep], mated[sweep], below[sweep], across[sweep]
        own = own_u.at[sweep]

        def entry(o):
            return block.at[o], got_sem.at[sweep, o]

        def await_entry(o):
            arrived(*entry(o), me >= o)

        send(sweep, 0, own, *entry(4), up, has_up)
        send(sweep, 1, own, *entry(2), pair, even_chip)
        send(sweep, 2, own, *entry(1), mate, even_core)

        @pl.loop(0, slots)
        def _(j):
            if sweep == 0:
                pltpu.make_async_copy(couplings_hbm.at[j], couplings.at[j], load_sem.at[j]).wait()

            @pl.loop(0, tiles)
            def _(c):
                cols = columns(c)
                acc = lax.dot_general(own[...], couplings[j, 0, :, cols], NN, preferred_element_type=jnp.float32)
                acc += lax.dot_general(own_v[...], couplings[j, 1, :, cols], NN, preferred_element_type=jnp.float32)
                behind[j, :, cols] = acc.astype(jnp.bfloat16)

        for number, o in enumerate((7, 5, 3, 1)):
            i = o // 2
            part[o - 1] = behind[listed[o - 1]]
            slot = i + 1 - core
            send(sweep, 8 + number, part.at[o - 1], mates.at[slot], mated_sem.at[sweep, slot], mate)
        for o in (6, 8, 2, 4):
            part[o - 1] = behind[listed[o - 1]]

        def add(o, ref):
            total = part[o - 1].astype(jnp.float32) + ref[...].astype(jnp.float32)
            part[o - 1] = total.astype(jnp.bfloat16)

        await_entry(4)
        send(sweep, 3, block.at[4], *entry(2), pair, has_down & jnp.logical_not(even_chip))
        send(sweep, 4, block.at[4], *entry(8), up, has_up & has_down)

        arrived(mates.at[3], mated_sem.at[sweep, 3])
        arrived(mates.at[4 * core], mated_sem.at[sweep, 4 * core])
        arrived(mates.at[1], mated_sem.at[sweep, 1])
        arrived(mates.at[2], mated_sem.at[sweep, 2])
        add(6, mates.at[3])
        send(sweep, 12, part.at[5], lows.at[0], below_sem.at[sweep, 0], down, has_down)
        add(8, mates.at[4])
        send(sweep, 13, part.at[7], lows.at[1], below_sem.at[sweep, 1], down, has_down)
        add(2, mates.at[1])
        add(4, mates.at[2])

        await_entry(2)
        send(sweep, 5, block.at[2], *entry(6), up, has_up & (me >= 2))
        to_mate = 1 - core
        send(sweep, 6, block.at[2], *entry(1 + 2 * to_mate), mate, me >= 2)
        send(sweep, 7, block.at[4], *entry(3 + 2 * to_mate), mate, me >= 4)

        @pl.when(has_up)
        def _():
            arrived(lows.at[0], below_sem.at[sweep, 0])
            add(2, lows.at[0])

        send(sweep, 14, part.at[1], over, across_sem.at[sweep], pair)

        @pl.when(has_up)
        def _():
            arrived(lows.at[1], below_sem.at[sweep, 1])
            add(4, lows.at[1])

        @pl.when(jnp.logical_not(even_chip))
        def _():
            arrived(over, across_sem.at[sweep])
            add(4, over)

        send(sweep, 15, part.at[3], lows.at[2], below_sem.at[sweep, 2], down, has_down)

        await_entry(8)
        send(sweep, 17, block.at[8], *entry(7), mate, (me >= 8) & jnp.logical_not(even_core))
        await_entry(6)
        send(sweep, 16, block.at[6], *entry(5 + 2 * to_mate), mate, me >= 6)
        for o in (1, 3, 5, 7):
            await_entry(o)

        for j in range(slots):
            taken = block[offsets[j]]
            staged_u[j] = taken
            staged_v[j, :half] = -taken[half:]
            staged_v[j, half:] = taken[:half]

        @pl.loop(0, tiles)
        def _(c):
            cols = columns(c)
            acc = jnp.zeros((height, TILE), jnp.float32)
            for j in range(slots):
                acc += lax.dot_general(staged_u[j], couplings[j, 0, cols, :], NT, preferred_element_type=jnp.float32)
                acc += lax.dot_general(staged_v[j], couplings[j, 1, cols, :], NT, preferred_element_type=jnp.float32)
            fields[:, cols] = incident_ref[:, cols] - acc

        arrived(lows.at[2], below_sem.at[sweep, 2], has_up)
        arrived(over, across_sem.at[sweep], even_chip)
        incoming = mates[0].astype(jnp.float32) + lows[2].astype(jnp.float32)
        incoming += jnp.where(even_chip, over[...].astype(jnp.float32), 0.0)
        right = (fields[...] - incoming).astype(jnp.bfloat16)
        right_u[...] = right
        right_v[:half] = -right[half:]
        right_v[half:] = right[:half]
        if sweep < ITERS - 1:
            solve(right_u, right_v, own_u.at[sweep + 1], own_v, False)
        else:
            solve(right_u, right_v, None, None, True)

    for copy, cond in sent:
        if cond is None:
            copy.wait_send()
        else:
            pl.when(cond)(copy.wait_send)


def body(incident, self_block_inverse, couplings, partners, basis_count):
    n = lax.axis_size("turb")
    _, _, rows, width = incident.shape
    slots = couplings.shape[1]
    height = 2 * rows
    block = (height, width)
    bf16 = jnp.bfloat16
    vmem = pl.BlockSpec(memory_space=pltpu.VMEM)
    smem = pl.BlockSpec(memory_space=pltpu.SMEM)
    anywhere = pl.BlockSpec(memory_space=pl.ANY)
    dma = pltpu.SemaphoreType.DMA
    out = pl.pallas_call(
        functools.partial(kernel, n),
        out_shape=jax.ShapeDtypeStruct(block, jnp.float32),
        in_specs=[smem, smem, vmem, anywhere, anywhere],
        out_specs=vmem,
        scratch_shapes=[
            pltpu.VMEM((2, width, width), bf16),
            pltpu.VMEM((slots, 2, width, width), bf16),
            pltpu.VMEM((ITERS,) + block, bf16),
            pltpu.VMEM(block, bf16),
            pltpu.VMEM(block, jnp.float32),
            pltpu.VMEM((8, 128), jnp.float32),
            pltpu.VMEM((slots,) + block, bf16),
            pltpu.VMEM((slots,) + block, bf16),
            pltpu.VMEM(block, bf16),
            pltpu.VMEM(block, bf16),
            pltpu.VMEM((slots + 1,) + block, bf16),
            pltpu.VMEM((REACH + 1,) + block, bf16),
            pltpu.VMEM((REACH + 1,) + block, bf16),
            pltpu.VMEM((REACH,) + block, bf16),
            pltpu.VMEM((REACH,) + block, bf16),
            pltpu.VMEM((5,) + block, bf16),
            pltpu.VMEM((5,) + block, bf16),
            pltpu.VMEM((3,) + block, bf16),
            pltpu.VMEM((3,) + block, bf16),
            pltpu.VMEM(block, bf16),
            pltpu.VMEM(block, bf16),
            dma((slots + 1,)),
            dma((ITERS, 18)),
            dma((ITERS, REACH + 1)),
            dma((ITERS, 5)),
            dma((ITERS, 3)),
            dma((ITERS,)),
        ],
        compiler_params=pltpu.CompilerParams(
            collective_id=0, has_side_effects=True, vmem_limit_bytes=58 * 2**20
        ),
        cost_estimate=pl.CostEstimate(
            flops=2 * (ITERS + 1 + 2 * ITERS * slots) * 2 * height * width * width,
            bytes_accessed=(slots + 1) * 4 * width * width,
            transcendentals=0,
        ),
    )(partners, basis_count, incident.reshape(block), self_block_inverse[0], couplings[0])
    return out.reshape(incident.shape)


def solution(mesh):
    placed = (
        P(("group", "turb"), None, None, None),
        P(("group", "turb"), None, None, None),
        P(("group", "turb"), None, None, None, None),
        P(("group", "turb"), None),
        P(("group", "turb")),
    )
    return jax.shard_map(
        body,
        mesh=mesh,
        in_specs=placed,
        out_specs=P(("group", "turb"), None, None, None),
        check_vma=False,
    )
```

```python
import functools

import jax
import jax.numpy as jnp
from jax import lax
from jax.experimental import pallas as pl
from jax.experimental.pallas import tpu as pltpu
from jax.sharding import PartitionSpec as P

ITERS = 2
REACH = 8
TILE = 512
PARTS = 4
UNROLL = True
ORDER = (
    "B0 B1 40 A0",
    "B2 41 A1 B3",
    "42 A2 20 43",
    "A3 21 Y0 22",
    "Y1 23 Y2 M0",
    "C0 Y3 M1 C1",
    "F0 C2 M2 F1",
    "C3 M3 F2 F3",
    "R0 R1 R2 R3",
)
MESH = pl.DeviceIdType.MESH
NT = (((1,), (1,)), ((), ()))
NN = (((1,), (0,)), ((), ()))


def kernel(n, partners_ref, count_ref, incident_ref, inverse_hbm, couplings_hbm, out_ref, *scratch):
    (
        inverse, couplings, own, own_v, own_parts, fields, staged_u, staged_v, right_u, right_v, behind,
        parts, mated, below, across, load_sem, send_sem, got_sem, mated_sem, below_sem, across_sem,
    ) = scratch[:21]
    got = [scratch[21 + sweep * PARTS:21 + (sweep + 1) * PARTS] for sweep in range(ITERS)]
    slots = couplings_hbm.shape[0]
    height, width = incident_ref.shape
    half = height // 2
    wide = width // PARTS
    me = lax.axis_index("turb")
    core = lax.rem(me, 2)
    odd_chip = lax.rem(me // 2, 2)
    even_core, even_chip = core == 0, odd_chip == 0
    mate = me + 1 - 2 * core
    pair = me + 2 - 4 * odd_chip
    has_up = me + 4 < n
    has_down = me >= 4
    up = jnp.where(has_up, me + 4, me)
    down = jnp.where(has_down, me - 4, me)

    def cols(c):
        return pl.ds(c * wide, wide)

    load_inverse = [
        pltpu.make_async_copy(inverse_hbm.at[:, cols(c)], inverse.at[:, cols(c)], load_sem.at[0, c])
        for c in range(PARTS)
    ]
    load_couplings = [
        pltpu.make_async_copy(couplings_hbm.at[:, :, :, cols(c)], couplings.at[:, :, :, cols(c)], load_sem.at[1, c])
        for c in range(PARTS)
    ]
    for copy in load_inverse:
        copy.start()

    empty = jnp.zeros((height, wide), jnp.bfloat16)
    for sweep in range(ITERS):
        for c in range(PARTS):
            for o in range(REACH + 1):
                got[sweep][c][o] = empty
            mated[sweep, c, 0] = empty
            mated[sweep, c, 4] = empty
            below[sweep, c, 2] = empty
    behind[slots] = empty

    barrier = pltpu.get_barrier_semaphore()

    def greet(other):
        pl.semaphore_signal(barrier, inc=1, device_id={"turb": other}, device_id_type=MESH)

    greet(mate)
    greet(pair)
    pl.when(has_up)(lambda: greet(up))
    pl.when(has_down)(lambda: greet(down))

    count = count_ref[0]
    offsets = []
    for j in range(slots):
        partner = partners_ref[0, j]
        offsets.append(jnp.clip(jnp.where(partner >= 0, me - partner, 0), 0, REACH))
    listed = []
    for o in range(1, REACH + 1):
        place = jnp.int32(slots)
        for j in range(slots):
            place = jnp.where(offsets[j] == o, j, place)
        listed.append(place)

    def set_right(c, right):
        right_u[:, cols(c)] = right
        right_v[:half, cols(c)] = -right[half:]
        right_v[half:, cols(c)] = right[:half]

    def solved(c):
        acc = lax.dot_general(right_u[...], inverse[0, cols(c), :], NT, preferred_element_type=jnp.float32)
        acc += lax.dot_general(right_v[...], inverse[1, cols(c), :], NT, preferred_element_type=jnp.float32)
        position = lax.broadcasted_iota(jnp.int32, (height, wide), 1) + c * wide
        return acc * (position < count).astype(jnp.float32)

    sent = []

    def send(sweep, c, number, src, dst, arrival, device, cond=None):
        copy = pltpu.make_async_remote_copy(
            src_ref=src, dst_ref=dst, send_sem=send_sem.at[sweep, c, number], recv_sem=arrival,
            device_id={"turb": device}, device_id_type=MESH,
        )
        sent.append((copy, cond))
        if cond is None:
            copy.start()
        else:
            pl.when(cond)(copy.start)

    def arrived(dst, arrival, cond=None):
        copy = pltpu.make_async_remote_copy(
            src_ref=dst, dst_ref=dst, send_sem=send_sem.at[0, 0, 0], recv_sem=arrival,
            device_id={"turb": mate}, device_id_type=MESH,
        )
        if cond is None:
            copy.wait_recv()
        else:
            pl.when(cond)(copy.wait_recv)

    def entry(sweep, c, o):
        return got[sweep][c].at[o], got_sem.at[sweep, c, o]

    def solve_and_send(sweep, c):
        rounded = solved(c).astype(jnp.bfloat16)
        own[:, cols(c)] = rounded
        own_v[:half, cols(c)] = -rounded[half:]
        own_v[half:, cols(c)] = rounded[:half]
        own_parts[sweep, c] = rounded
        if sweep == 0 and c == 0:
            pl.semaphore_wait(barrier, 2 + has_up.astype(jnp.int32) + has_down.astype(jnp.int32))
        src = own_parts.at[sweep, c]
        send(sweep, c, 0, src, *entry(sweep, c, 4), up, has_up)
        send(sweep, c, 1, src, *entry(sweep, c, 2), pair, even_chip)
        send(sweep, c, 2, src, *entry(sweep, c, 1), mate, even_core)

    for c in range(PARTS):
        set_right(c, incident_ref[:, cols(c)].astype(jnp.bfloat16))
    for c in range(PARTS):
        load_inverse[c].wait()
        load_couplings[c].start()
        solve_and_send(0, c)

    to_mate = 1 - core
    for sweep in range(ITERS):

        def await_entry(c, o):
            arrived(*entry(sweep, c, o), me >= o)

        def add(c, o, value):
            total = parts[sweep, c, o - 1].astype(jnp.float32) + value.astype(jnp.float32)
            parts[sweep, c, o - 1] = total.astype(jnp.bfloat16)

        def low(c, i):
            return below.at[sweep, c, i], below_sem.at[sweep, c, i]

        def over(c):
            return across.at[sweep, c], across_sem.at[sweep, c]

        def transposed(c):
            if sweep == 0:
                load_couplings[c].wait()

            @pl.loop(0, slots, unroll=UNROLL)
            def _(j):
                acc = lax.dot_general(own[...], couplings[j, 0, :, cols(c)], NN, preferred_element_type=jnp.float32)
                acc += lax.dot_general(own_v[...], couplings[j, 1, :, cols(c)], NN, preferred_element_type=jnp.float32)
                behind[j] = acc.astype(jnp.bfloat16)

            for number, o in enumerate((7, 5, 3, 1)):
                parts[sweep, c, o - 1] = behind[listed[o - 1]]
                slot = o // 2 + 1 - core
                send(
                    sweep, c, 8 + number, parts.at[sweep, c, o - 1], mated.at[sweep, c, slot],
                    mated_sem.at[sweep, c, slot], mate,
                )
            for o in (6, 8, 2, 4):
                parts[sweep, c, o - 1] = behind[listed[o - 1]]

        def join_mate(c):
            for slot in (3, 4 * core, 1, 2):
                arrived(mated.at[sweep, c, slot], mated_sem.at[sweep, c, slot])
            add(c, 6, mated[sweep, c, 3])
            send(sweep, c, 12, parts.at[sweep, c, 5], *low(c, 0), down, me >= 6)
            add(c, 8, mated[sweep, c, 4])
            send(sweep, c, 13, parts.at[sweep, c, 7], *low(c, 1), down, me >= 8)
            add(c, 2, mated[sweep, c, 1])
            add(c, 4, mated[sweep, c, 2])

        def relay_four(c):
            await_entry(c, 4)
            held = entry(sweep, c, 4)[0]
            send(sweep, c, 3, held, *entry(sweep, c, 2), pair, has_down & jnp.logical_not(even_chip))
            send(sweep, c, 4, held, *entry(sweep, c, 8), up, has_up & has_down)
            send(sweep, c, 7, held, *entry(sweep, c, 3 + 2 * to_mate), mate, me >= 4)

        def relay_two(c):
            await_entry(c, 2)
            held = entry(sweep, c, 2)[0]
            send(sweep, c, 5, held, *entry(sweep, c, 6), up, has_up & (me >= 2))
            send(sweep, c, 6, held, *entry(sweep, c, 1 + 2 * to_mate), mate, me >= 2)

        def relay_rest(c):
            await_entry(c, 8)
            send(
                sweep, c, 17, entry(sweep, c, 8)[0], *entry(sweep, c, 7), mate,
                (me >= 8) & jnp.logical_not(even_core),
            )
            await_entry(c, 6)
            send(sweep, c, 16, entry(sweep, c, 6)[0], *entry(sweep, c, 5 + 2 * to_mate), mate, me >= 6)

        def pass_across(c):
            @pl.when(has_up & (me >= 2))
            def _():
                arrived(*low(c, 0))
                add(c, 2, below[sweep, c, 0])

            send(sweep, c, 14, parts.at[sweep, c, 1], *over(c), pair)

        def pass_down(c):
            @pl.when(has_up & has_down)
            def _():
                arrived(*low(c, 1))
                add(c, 4, below[sweep, c, 1])

            @pl.when(jnp.logical_not(even_chip))
            def _():
                arrived(*over(c))
                add(c, 4, across[sweep, c])

            send(sweep, c, 15, parts.at[sweep, c, 3], *low(c, 2), down, has_down)

        def forward(c):
            for o in (1, 3, 5, 7):
                await_entry(c, o)
            for j in range(slots):
                taken = got[sweep][c][offsets[j]]
                staged_u[j] = taken
                staged_v[j, :half] = -taken[half:]
                staged_v[j, half:] = taken[:half]

            @pl.loop(0, width // TILE)
            def _(r):
                rows = pl.ds(pl.multiple_of(r * TILE, TILE), TILE)
                acc = jnp.zeros((height, TILE), jnp.float32)
                for j in range(slots):
                    acc += lax.dot_general(
                        staged_u[j], couplings[j, 0, rows, cols(c)], NT, preferred_element_type=jnp.float32
                    )
                    acc += lax.dot_general(
                        staged_v[j], couplings[j, 1, rows, cols(c)], NT, preferred_element_type=jnp.float32
                    )
                before = incident_ref if c == 0 else fields
                fields[:, rows] = before[:, rows] - acc

        def finish(c):
            arrived(*low(c, 2), has_up)
            arrived(*over(c), even_chip)
            incoming = mated[sweep, c, 0].astype(jnp.float32) + below[sweep, c, 2].astype(jnp.float32)
            incoming += jnp.where(even_chip, across[sweep, c].astype(jnp.float32), 0.0)
            set_right(c, (fields[:, cols(c)] - incoming).astype(jnp.bfloat16))

        stages = {
            "B": transposed, "A": join_mate, "4": relay_four, "2": relay_two, "M": relay_rest,
            "Y": pass_across, "C": pass_down, "F": forward, "R": finish,
        }
        for step in " ".join(ORDER).split():
            stages[step[0]](int(step[1:]))
        for c in range(PARTS):
            if sweep < ITERS - 1:
                solve_and_send(sweep + 1, c)
            else:
                out_ref[:, cols(c)] = solved(c)

    for copy, cond in sent:
        if cond is None:
            copy.wait_send()
        else:
            pl.when(cond)(copy.wait_send)


def body(incident, self_block_inverse, couplings, partners, basis_count):
    n = lax.axis_size("turb")
    _, _, rows, width = incident.shape
    slots = couplings.shape[1]
    height = 2 * rows
    block, part = (height, width), (height, width // PARTS)
    bf16 = jnp.bfloat16
    vmem = pl.BlockSpec(memory_space=pltpu.VMEM)
    smem = pl.BlockSpec(memory_space=pltpu.SMEM)
    anywhere = pl.BlockSpec(memory_space=pl.ANY)
    dma = pltpu.SemaphoreType.DMA
    out = pl.pallas_call(
        functools.partial(kernel, n),
        out_shape=jax.ShapeDtypeStruct(block, jnp.float32),
        in_specs=[smem, smem, vmem, anywhere, anywhere],
        out_specs=vmem,
        scratch_shapes=[
            pltpu.VMEM((2, width, width), bf16),
            pltpu.VMEM((slots, 2, width, width), bf16),
            pltpu.VMEM(block, bf16),
            pltpu.VMEM(block, bf16),
            pltpu.VMEM((ITERS, PARTS) + part, bf16),
            pltpu.VMEM(block, jnp.float32),
            pltpu.VMEM((slots,) + part, bf16),
            pltpu.VMEM((slots,) + part, bf16),
            pltpu.VMEM(block, bf16),
            pltpu.VMEM(block, bf16),
            pltpu.VMEM((slots + 1,) + part, bf16),
            pltpu.VMEM((ITERS, PARTS, REACH) + part, bf16),
            pltpu.VMEM((ITERS, PARTS, 5) + part, bf16),
            pltpu.VMEM((ITERS, PARTS, 3) + part, bf16),
            pltpu.VMEM((ITERS, PARTS) + part, bf16),
            dma((2, PARTS)),
            dma((ITERS, PARTS, 18)),
            dma((ITERS, PARTS, REACH + 1)),
            dma((ITERS, PARTS, 5)),
            dma((ITERS, PARTS, 3)),
            dma((ITERS, PARTS)),
        ] + [pltpu.VMEM((REACH + 1,) + part, bf16) for _ in range(ITERS * PARTS)],
        compiler_params=pltpu.CompilerParams(
            collective_id=0, has_side_effects=True, vmem_limit_bytes=58 * 2**20
        ),
        cost_estimate=pl.CostEstimate(
            flops=2 * (ITERS + 1 + 2 * ITERS * slots) * 2 * height * width * width,
            bytes_accessed=(slots + 1) * 4 * width * width,
            transcendentals=0,
        ),
    )(partners, basis_count, incident.reshape(block), self_block_inverse[0], couplings[0])
    return out.reshape(incident.shape)


def solution(mesh):
    placed = (
        P(("group", "turb"), None, None, None),
        P(("group", "turb"), None, None, None),
        P(("group", "turb"), None, None, None, None),
        P(("group", "turb"), None),
        P(("group", "turb")),
    )
    return jax.shard_map(
        body,
        mesh=mesh,
        in_specs=placed,
        out_specs=P(("group", "turb"), None, None, None),
        check_vma=False,
    )
```
